256 devices in a mesh: chan: 64 (over y_hi, x, z), win: 4 (over y_lo, core).
Axes of the slice: x: 4, y: 4 (y_hi: 2, y_lo: 2; y = y_hi * 2 + y_lo), z: 8, core: 2. Of those that a mesh axis runs over, the one named last changes fastest.
Arguments:
- spectra: bfloat16 [64, 128, 128, 2, 128], P('chan', None, 'win'), may hold values from -6 to 6
- counts: int32 [128, 64], P('win'), may hold values from 1 to 256
- partner: int32 [2, 64], replicated, may hold values from 0 to 63, as said below
Outputs:
- cross: bfloat16 [64, 2, 128, 128, 256], P('win', None, 'chan')
The draws below stay inside these ranges and needn't reach their ends.
Inputs may be any that keep to these rules, and one draw needn't show every extreme that they name: Each row of partner is one cycle through all 64 blocks: a permutation with no block its own partner and no two blocks each other's partners.
All inputs are finite; a program needn't handle non-finite values.
Results may differ from the reference program's by a relative error of at most 0.015.
Values may be sent and summed in bfloat16 or wider, within the bound.
No kernel may reach another device: no remote copies, remote signals or barrier semaphores. Data moves between devices by JAX's collectives and lax.ppermute only.
A program may use at most 128 MiB of HBM per device.

```python
import jax
import jax.numpy as jnp
from jax import lax

CB = 128
F = 128
W_DEV = 32
R = 2
NSAMP = 256
BLOCKS = 64
W_TOTAL = 128
N_WIN = 4


def draw_partner(key, part):
    rows = []
    for round_index in range(R):
        order = jax.random.permutation(jax.random.fold_in(key, round_index + 11), BLOCKS).astype(jnp.int32)
        following = jnp.roll(order, -1)
        row = jnp.zeros((BLOCKS,), jnp.int32).at[order].set(following)
        rows.append(row)
    return jnp.stack(rows)


def set_ends(drawn, rng, least, high):
    longest = drawn.shape.index(max(drawn.shape))
    spots = []
    for shift in (0, 1):
        where = [jax.random.randint(jax.random.fold_in(rng, axis), (), 0, length) for axis, length in enumerate(drawn.shape)]
        where[longest] = (where[longest] + shift) % drawn.shape[longest]
        spots.append(tuple(where))
    return drawn.at[spots[0]].set(least).at[spots[1]].set(high)


def levels(own_key, dims, shards, smallest, high):
    gain, own = 1.0, jax.random.fold_in(own_key, 6)
    for dim, blocks in shards:
        steps = jnp.exp(jax.random.uniform(jax.random.fold_in(own, dim), (blocks,), jnp.float32, smallest / len(shards), high / len(shards)))
        gain = gain * jnp.repeat(steps, dims[dim] // blocks).reshape([-1 if axis == dim else 1 for axis in range(len(dims))])
    return gain


def bell_draw(key, shape, spread, bound, shards=(), held_as=jnp.bfloat16):
    values = spread * jax.random.normal(key, shape, jnp.float32)
    if shards:
        values = values * levels(key, shape, shards, -0.22, 0.18)
    return jnp.clip(values, -bound, bound).astype(held_as)


def setup_inputs(seed: int = 0) -> dict:
    keys = jax.random.split(jax.random.key(seed), 4)
    return {
        "spectra": bell_draw(keys[0], (BLOCKS, F, W_TOTAL, 2, CB), 1.0, 6.0, ((0, 64), (2, 4))),
        "counts": set_ends(jax.random.randint(keys[1], (W_TOTAL, BLOCKS), 1, NSAMP + 1), jax.random.fold_in(keys[1], 1), 1, NSAMP).astype(jnp.int32),
        "partner": draw_partner(jax.random.fold_in(keys[3], 71), 0),
    }


EPS = 1e-06

def reference(spectra, counts, partner):
    values = spectra.astype(jnp.float32)
    power = lax.optimization_barrier(jnp.mean(lax.optimization_barrier(jnp.sum(values * values, axis=3)), axis=1))
    whitened = (values * lax.rsqrt(power + EPS)[:, None, :, None, :]).astype(jnp.bfloat16)
    blocks = whitened.reshape(BLOCKS, F, N_WIN, W_DEV, 2, CB)
    tallies = counts.astype(jnp.float32).T
    weight = jnp.minimum(tallies[None], jnp.take(tallies, partner, axis=0)) / NSAMP
    norm = jnp.sqrt(lax.optimization_barrier(jnp.sum(weight * weight, axis=2)))
    grouped = weight.reshape(R, BLOCKS, N_WIN, W_DEV)

    def one_block(index):
        own = lax.dynamic_index_in_dim(blocks, index, 0, keepdims=False)
        mates = jnp.take(blocks, partner[:, index], axis=0)
        scale = grouped[:, index]
        weighted = (scale[:, None, :, :, None, None] * own[None].astype(jnp.float32)).astype(jnp.bfloat16)
        rotated = jnp.stack([-mates[..., 1, :], mates[..., 0, :]], axis=-2)
        paired = jnp.stack([mates, rotated], axis=-2)
        partial_value = jnp.einsum('rfgwkc,rfgwkod->grfcod', weighted.astype(jnp.float32), paired.astype(jnp.float32))
        partial_value = lax.optimization_barrier(partial_value.astype(jnp.bfloat16))
        total = lax.optimization_barrier(jnp.sum(partial_value.astype(jnp.float32), axis=0))
        result = total / norm[:, index][:, None, None, None, None]
        return result.astype(jnp.bfloat16).reshape(R, F, CB, 2 * CB)
    return lax.map(one_block, jnp.arange(BLOCKS))
```

```python
import functools

import jax
import jax.numpy as jnp
from jax import lax
from jax.experimental import pallas as pl
from jax.experimental.pallas import tpu as pltpu
from jax.sharding import PartitionSpec as P

NSAMP = 256
EPS = 1e-06


def whiten_kernel(x_ref, first_ref, second_ref):
    bins, rows, width = x_ref.shape
    step = 4

    def add(i, total):
        for j in range(step):
            values = x_ref[i * step + j].astype(jnp.float32)
            total = total + values * values
        return total

    total = lax.fori_loop(0, bins // step, add, jnp.zeros((rows, width), jnp.float32))
    even = lax.broadcasted_iota(jnp.int32, (rows, width), 0) % 2 == 0
    other = jnp.where(even, pltpu.roll(total, rows - 1, 0), pltpu.roll(total, 1, 0))
    scale = lax.rsqrt((total + other) / bins + EPS)

    def put(i, carry):
        for j in range(step):
            first_ref[i * step + j] = (x_ref[(i * step + j) * 2].astype(jnp.float32) * scale).astype(first_ref.dtype)
            second_ref[i * step + j] = (x_ref[(i * step + j) * 2 + 1].astype(jnp.float32) * scale).astype(first_ref.dtype)
        return carry

    lax.fori_loop(0, bins // 2 // step, put, 0)


def whiten(spectra):
    bins, rows, width = spectra.shape
    half = jax.ShapeDtypeStruct((bins // 2, rows, width), spectra.dtype)
    return pl.pallas_call(
        whiten_kernel,
        out_shape=(half, half),
        in_specs=[pl.BlockSpec(memory_space=pltpu.VMEM)],
        out_specs=[pl.BlockSpec(memory_space=pltpu.VMEM)] * 2,
        compiler_params=pltpu.CompilerParams(vmem_limit_bytes=24 << 20),
        name="whiten",
    )(spectra)


def stack_kernel(chosen, mates_ref, first_ref, weight_ref, norm_ref, *refs):
    sources, out_ref = refs[:4], refs[-1]
    n = pl.program_id(0)
    own = jnp.concatenate([s[first_ref[0] + n] for s in sources], axis=0)
    rows, width = own.shape
    real = own.astype(jnp.float32).T
    even = lax.broadcasted_iota(jnp.int32, (width, rows), 1) % 2 == 0
    turned = jnp.where(even, pltpu.roll(real, rows - 1, 1), -pltpu.roll(real, 1, 1))
    both = jnp.concatenate([real, turned], axis=0)
    for r in range(2):
        mate = jnp.concatenate([s[mates_ref[r * chosen + n]] for s in sources], axis=0)
        left = (both * weight_ref[0, r][None, :]).astype(jnp.bfloat16)
        total = lax.dot_general(left, mate, (((1,), (0,)), ((), ())), preferred_element_type=jnp.float32)
        total = (total * (1.0 / norm_ref[r * chosen + n])).astype(out_ref.dtype)
        out_ref[0, r, 0, :, :width] = total[:width]
        out_ref[0, r, 0, :, width:] = total[width:]


def stack(which, sources, mates, first, weight, norm, into):
    chosen, rounds, rows = weight.shape
    width = sources[0].shape[-1]
    out = jax.ShapeDtypeStruct((chosen, rounds, 2, width, 2 * width), jnp.bfloat16)
    smem = pl.BlockSpec(memory_space=pltpu.SMEM)
    vmem = pl.BlockSpec(memory_space=pltpu.VMEM)
    more = () if into is None else (into,)
    return pl.pallas_call(
        functools.partial(stack_kernel, chosen),
        out_shape=out,
        grid=(chosen,),
        in_specs=[smem, smem, pl.BlockSpec((1, rounds, rows), lambda n: (n, 0, 0)), smem]
        + [vmem] * 4
        + [pl.BlockSpec(memory_space=pl.ANY)] * len(more),
        out_specs=pl.BlockSpec((1, rounds, 1, width, 2 * width), lambda n: (n, 0, which, 0, 0)),
        input_output_aliases={8: 0} if more else {},
        compiler_params=pltpu.CompilerParams(vmem_limit_bytes=24 << 20),
        cost_estimate=pl.CostEstimate(flops=2 * chosen * rounds * 2 * width * rows * width, bytes_accessed=8 << 20, transcendentals=0),
        name="stack" + str(which),
    )(mates, first, weight, norm, *sources, *more)


def per_device(spectra, counts, partner):
    bins, windows, parts, width = spectra.shape[1:]
    nblocks = partner.shape[1]
    rounds = partner.shape[0]
    groups = lax.axis_size("win")
    chosen = nblocks // groups
    me = lax.axis_index("win")
    first = me * chosen

    def swap(x, mask):
        return lax.ppermute(x, "win", [(i, i ^ mask) for i in range(groups)])

    halves = whiten(spectra.reshape(bins, windows * parts, width))
    tallies = [counts, swap(counts, 2), swap(counts, 1), swap(counts, 3)]

    mixed = [lax.all_to_all(h, "chan", split_axis=0, concat_axis=0, tiled=True) for h in halves]
    gathered = []
    for m in mixed:
        y = swap(m, 2)
        gathered.append((m, y, swap(m, 1), swap(y, 1)))

    columns = jnp.concatenate(tallies, axis=0).astype(jnp.float32)
    mine = lax.dynamic_slice_in_dim(partner, first, chosen, 1)
    one_hot = (mine.reshape(rounds * chosen, 1) == jnp.arange(nblocks, dtype=jnp.int32)[None]).astype(jnp.float32)
    own_hot = (first + jnp.arange(chosen, dtype=jnp.int32)[:, None] == jnp.arange(nblocks, dtype=jnp.int32)[None]).astype(jnp.float32)
    pick = functools.partial(jnp.einsum, "nb,wb->nw", precision=lax.Precision.HIGHEST)
    theirs = pick(one_hot, columns).reshape(rounds, chosen, -1)
    ours = pick(own_hot, columns)
    weight = jnp.minimum(ours[None], theirs) / NSAMP
    norm = jnp.sqrt(jnp.sum(weight * weight, axis=2)).reshape(rounds * chosen)
    wide = jnp.repeat(jnp.transpose(weight, (1, 0, 2)), parts, axis=2)

    result = None
    for which in range(2):
        result = stack(which, gathered[which], mine.reshape(-1), first.reshape(1).astype(jnp.int32), wide, norm, result)
    return result


def solution(mesh):
    placed = (P("chan", None, "win", None, None), P("win", None), P())
    return jax.shard_map(
        per_device,
        mesh=mesh,
        in_specs=placed,
        out_specs=P("win", None, "chan", None, None),
        check_vma=False,
    )
```

```python
import functools

import jax
import jax.numpy as jnp
from jax import lax
from jax.experimental import pallas as pl
from jax.experimental.pallas import tpu as pltpu
from jax.sharding import Mesh, PartitionSpec as P

NSAMP = 256
EPS = 1e-06
UNROLL = 8


def whiten_kernel(side_ref, x_ref, near_ref, early_ref, late_ref):
    bins, rows, width = x_ref.shape
    half = bins // 2
    more = early_ref.shape[1] - rows
    step = 4

    def add(i, total):
        for j in range(step):
            values = x_ref[i * step + j].astype(jnp.float32)
            total = total + values * values
        return total

    total = lax.fori_loop(0, bins // step, add, jnp.zeros((rows, width), jnp.float32))
    first = lax.broadcasted_iota(jnp.int32, (rows, width), 0) % 2 == 0
    other = jnp.where(first, pltpu.roll(total, rows - 1, 0), pltpu.roll(total, 1, 0))
    scale = lax.rsqrt((total + other) / bins + EPS)
    near = side_ref[0] * half
    far = half - near

    def put(i, carry):
        for j in range(step):
            at = i * step + j
            for which in range(2):
                near_ref[at, which] = (x_ref[near + 2 * at + which].astype(jnp.float32) * scale).astype(near_ref.dtype)
            early_ref[at, :rows] = (x_ref[far + 2 * at].astype(jnp.float32) * scale).astype(early_ref.dtype)
            odd = (x_ref[far + 2 * at + 1].astype(jnp.float32) * scale).astype(early_ref.dtype)
            early_ref[at, rows:] = odd[:more]
            late_ref[at] = odd[more:]
        return carry

    lax.fori_loop(0, half // 2 // step, put, 0)


def whiten(side, spectra):
    bins, rows, width = spectra.shape
    places = bins // 4
    vmem = pl.BlockSpec(memory_space=pltpu.VMEM)
    return pl.pallas_call(
        whiten_kernel,
        out_shape=[
            jax.ShapeDtypeStruct(shape, spectra.dtype)
            for shape in ((places, 2, rows, width), (places, rows + rows // 2, width), (places, rows // 2, width))
        ],
        in_specs=[pl.BlockSpec(memory_space=pltpu.SMEM), vmem],
        out_specs=[vmem] * 3,
        compiler_params=pltpu.CompilerParams(vmem_limit_bytes=16 << 20),
        name="whiten",
    )(side, spectra)


def turn_matrix(rows):
    i = lax.broadcasted_iota(jnp.int32, (rows, rows), 0)
    j = lax.broadcasted_iota(jnp.int32, (rows, rows), 1)
    plus = (i == j + 1) & (j % 2 == 0)
    minus = (i == j - 1) & (j % 2 == 1)
    return (plus.astype(jnp.float32) - minus.astype(jnp.float32)).astype(jnp.bfloat16)


def stack_kernel(which, side_ref, first_ref, mates_ref, weight_ref, norm_ref, *refs):
    near, early, late, out_ref = refs[:4], refs[4:8], refs[8:12], refs[-1]
    chosen, rounds = weight_ref.shape[:2]
    half, _, rows, width = near[0].shape
    side = side_ref[0]

    def block(b):
        mine = b // half == side
        at = b % half
        parts = []
        for t in range(4):
            if which == 0:
                far = early[t ^ 2][at, :rows]
            else:
                far = jnp.concatenate([early[t ^ 2][at, rows:], late[t ^ 2][at]], axis=0)
            parts.append(jnp.where(mine, near[t][at, which], far))
        return jnp.concatenate(parts, axis=0)

    turn = turn_matrix(4 * rows)
    for u in range(UNROLL):
        n = pl.program_id(0) * UNROLL + u
        own = block(first_ref[0] + n).T
        turned = jnp.dot(own, turn, preferred_element_type=jnp.float32).astype(own.dtype)
        left = jnp.concatenate([own, turned], axis=0)
        right = jnp.concatenate([block(mates_ref[r * chosen + n]) * weight_ref[n, r] for r in range(rounds)], axis=1)
        both = jnp.dot(left, right, preferred_element_type=jnp.float32)
        for r in range(rounds):
            total = (both[:, r * width : (r + 1) * width] * (1.0 / norm_ref[r * chosen + n])).astype(out_ref.dtype)
            out_ref[u, r, 0, :, :width] = total[:width]
            out_ref[u, r, 0, :, width:] = total[width:]


def stack(which, near, early, late, side, first, mates, weight, norm, into):
    chosen, rounds, rows, width = weight.shape
    out = jax.ShapeDtypeStruct((chosen, rounds, 2, width, 2 * width), jnp.bfloat16)
    smem = pl.BlockSpec(memory_space=pltpu.SMEM)
    vmem = pl.BlockSpec(memory_space=pltpu.VMEM)
    far = [*early, *late] if which else [*early]
    refs = [smem, smem, smem, vmem, smem] + [vmem] * (len(near) + len(far))
    more = () if into is None else (into,)
    return pl.pallas_call(
        functools.partial(stack_kernel, which),
        out_shape=out,
        grid=(chosen // UNROLL,),
        in_specs=refs + [pl.BlockSpec(memory_space=pl.ANY)] * len(more),
        out_specs=pl.BlockSpec((UNROLL, rounds, 1, width, 2 * width), lambda n: (n, 0, which, 0, 0)),
        input_output_aliases={len(refs): 0} if more else {},
        compiler_params=pltpu.CompilerParams(vmem_limit_bytes=24 << 20),
        cost_estimate=pl.CostEstimate(flops=20 * chosen * rounds * 2 * width * rows * width, bytes_accessed=8 << 20, transcendentals=0),
        name="stack" + str(which),
    )(side, first, mates, weight, norm, *near, *far, *more)


def per_device(spectra, counts, partner):
    bins, windows, parts, width = spectra.shape[1:]
    rounds, nblocks = partner.shape
    groups = lax.axis_size("yl") * lax.axis_size("core")
    chosen = nblocks // groups
    me = lax.axis_index(("yl", "core"))
    side = lax.axis_index("yh").reshape(1)
    first = me * chosen
    swap_pairs = [(0, 1), (1, 0)]
    after = lax.optimization_barrier

    def across(x):
        return lax.ppermute(x, "core", swap_pairs)

    def along(x):
        return lax.ppermute(x, "yl", swap_pairs)

    def hand_on(x):
        return lax.ppermute(x, ("yh", "yl"), [(0, 3), (3, 0), (1, 2), (2, 1)])

    shuffle = functools.partial(lax.all_to_all, axis_name=("x", "z"), split_axis=0, concat_axis=0, tiled=True)

    near, early, late = whiten(side, spectra.reshape(bins, windows * parts, width))
    early, late = hand_on(early), hand_on(late)
    beside = along(counts)
    tallies = (counts, across(counts), beside, across(beside))

    columns = jnp.concatenate(tallies, axis=0).astype(jnp.float32)
    mine = lax.dynamic_slice_in_dim(partner, first, chosen, 1)
    every = jnp.arange(nblocks, dtype=jnp.int32)
    theirs_hot = (mine.reshape(rounds * chosen, 1) == every[None]).astype(jnp.float32)
    ours_hot = (first + jnp.arange(chosen, dtype=jnp.int32)[:, None] == every[None]).astype(jnp.float32)
    pick = functools.partial(jnp.einsum, "nb,wb->nw", precision=lax.Precision.HIGHEST)
    theirs = pick(theirs_hot, columns).reshape(rounds, chosen, -1)
    ours = pick(ours_hot, columns)
    weight = jnp.minimum(ours[None], theirs) / NSAMP
    norm = jnp.sqrt(jnp.sum(weight * weight, axis=2)).reshape(rounds * chosen)
    wide = jnp.repeat(jnp.transpose(weight, (1, 0, 2)), parts, axis=2)
    wide = jnp.broadcast_to(wide.astype(jnp.bfloat16)[..., None], wide.shape + (width,))

    near = shuffle(near)
    near, early, late, wide, norm = after((near, early, late, wide, norm))
    near_beside = along(near)
    near = (near, across(near), near_beside, across(near_beside))
    early = shuffle(early)
    late, near = after((late, near))
    early_beside = along(early)
    late = shuffle(late)
    late, early_beside = after((late, early_beside))
    late_beside = along(late)

    operands = (side, first.reshape(1), mine.reshape(-1), wide, norm)
    early = (early, across(early), early_beside, across(early_beside))
    result = stack(0, near, early, None, *operands, None)
    late_beside, result = after((late_beside, result))
    late = (late, across(late), late_beside, across(late_beside))
    return stack(1, near, early, late, *operands, result)


def solution(mesh):
    split = Mesh(mesh.devices.reshape(2, 4, 8, 2, 2), ("yh", "x", "z", "yl", "core"))
    chan, win = ("yh", "x", "z"), ("yl", "core")
    return jax.shard_map(
        per_device,
        mesh=split,
        in_specs=(P(chan, None, win, None, None), P(win, None), P()),
        out_specs=P(win, None, chan, None, None),
        check_vma=False,
    )
```

```python
import functools

import jax
import jax.numpy as jnp
from jax import lax
from jax.experimental import pallas as pl
from jax.experimental.pallas import tpu as pltpu
from jax.sharding import Mesh, PartitionSpec as P

NSAMP = 256
EPS = 1e-06
UNROLL = 8


def whiten_kernel(side_ref, x_ref, near_ref, early_ref, late_ref):
    bins, rows, width = x_ref.shape
    half = bins // 2
    more = early_ref.shape[1] - rows
    step = 4

    def add(i, total):
        for j in range(step):
            values = x_ref[i * step + j].astype(jnp.float32)
            total = total + values * values
        return total

    total = lax.fori_loop(0, bins // step, add, jnp.zeros((rows, width), jnp.float32))
    first = lax.broadcasted_iota(jnp.int32, (rows, width), 0) % 2 == 0
    other = jnp.where(first, pltpu.roll(total, rows - 1, 0), pltpu.roll(total, 1, 0))
    scale = lax.rsqrt((total + other) / bins + EPS)
    near = side_ref[0] * half
    far = half - near

    def put(i, carry):
        for j in range(step):
            at = i * step + j
            for which in range(2):
                near_ref[at, which] = (x_ref[near + 2 * at + which].astype(jnp.float32) * scale).astype(near_ref.dtype)
            early_ref[at, :rows] = (x_ref[far + 2 * at].astype(jnp.float32) * scale).astype(early_ref.dtype)
            odd = (x_ref[far + 2 * at + 1].astype(jnp.float32) * scale).astype(early_ref.dtype)
            early_ref[at, rows:] = odd[:more]
            late_ref[at] = odd[more:]
        return carry

    lax.fori_loop(0, half // 2 // step, put, 0)


def whiten(side, spectra):
    bins, rows, width = spectra.shape
    places = bins // 4
    vmem = pl.BlockSpec(memory_space=pltpu.VMEM)
    return pl.pallas_call(
        whiten_kernel,
        out_shape=[
            jax.ShapeDtypeStruct(shape, spectra.dtype)
            for shape in ((places, 2, rows, width), (places, rows + rows // 2, width), (places, rows // 2, width))
        ],
        in_specs=[pl.BlockSpec(memory_space=pltpu.SMEM), vmem],
        out_specs=[vmem] * 3,
        compiler_params=pltpu.CompilerParams(vmem_limit_bytes=16 << 20),
        name="whiten",
    )(side, spectra)


def turn_matrix(rows):
    i = lax.broadcasted_iota(jnp.int32, (rows, rows), 0)
    j = lax.broadcasted_iota(jnp.int32, (rows, rows), 1)
    plus = (i == j + 1) & (j % 2 == 0)
    minus = (i == j - 1) & (j % 2 == 1)
    return (plus.astype(jnp.float32) - minus.astype(jnp.float32)).astype(jnp.bfloat16)


def stack_kernel(which, side_ref, first_ref, mates_ref, weight_ref, norm_ref, *refs):
    rounds = weight_ref.shape[2] // UNROLL
    chosen = norm_ref.shape[0] // rounds
    side = side_ref[0]
    if which == 0:
        near, early, (out_ref, near_kept, early_kept, sems) = refs[:4], refs[4:8], refs[8:]
        half, _, rows, width = near[0].shape
        moves = [(near[t].at[:, 1], near_kept.at[t], sems.at[0, t]) for t in range(4)]
        moves += [(early[t].at[:, pl.ds(rows, early_kept.shape[2])], early_kept.at[t], sems.at[1, t]) for t in range(4)]

        @pl.when(pl.program_id(0) == 0)
        def keep():
            for move in moves:
                pltpu.make_async_copy(*move).start()
    else:
        near_kept, early_kept, late, out_ref = refs[0], refs[1], refs[2:6], refs[-1]
        half, rows, width = near_kept.shape[1:]

    def block(b):
        mine = b // half == side
        at = b % half
        parts = []
        for t in range(4):
            if which == 0:
                parts.append(jnp.where(mine, near[t][at, 0], early[t ^ 2][at, :rows]))
            else:
                far = jnp.concatenate([early_kept[t ^ 2, at], late[t ^ 2][at]], axis=0)
                parts.append(jnp.where(mine, near_kept[t, at], far))
        return jnp.concatenate(parts, axis=0)

    def weighted(x, column):
        return (x.astype(jnp.float32) * weight_ref[0, :, column : column + 1]).astype(x.dtype)

    turn = turn_matrix(4 * rows)
    for u in range(UNROLL):
        n = pl.program_id(0) * UNROLL + u
        own = block(first_ref[0] + n).T
        turned = jnp.dot(own, turn, preferred_element_type=jnp.float32).astype(own.dtype)
        left = jnp.concatenate([own, turned], axis=0)
        right = jnp.concatenate([weighted(block(mates_ref[r * chosen + n]), u * rounds + r) for r in range(rounds)], axis=1)
        both = jnp.dot(left, right, preferred_element_type=jnp.float32)
        for r in range(rounds):
            total = (both[:, r * width : (r + 1) * width] * (1.0 / norm_ref[n * rounds + r])).astype(out_ref.dtype)
            out_ref[u, r, 0, :, :width] = total[:width]
            out_ref[u, r, 0, :, width:] = total[width:]


    if which == 0:

        @pl.when(pl.program_id(0) == pl.num_programs(0) - 1)
        def kept():
            for move in moves:
                pltpu.make_async_copy(*move).wait()


def stack(which, parts, side, first, mates, weight, norm, into):
    steps, rows, columns = weight.shape
    chosen, rounds, width = steps * UNROLL, columns // UNROLL, parts[0].shape[-1]
    shapes = [(chosen, rounds, 2, width, 2 * width)]
    smem = pl.BlockSpec(memory_space=pltpu.SMEM)
    vmem = pl.BlockSpec(memory_space=pltpu.VMEM)
    specs = [smem, smem, smem, pl.BlockSpec((1, rows, columns), lambda n: (n, 0, 0)), smem] + [vmem] * len(parts)
    if which == 0:
        places, _, some = parts[0].shape[:3]
        shapes += [(4, places, some, width), (4, places, parts[4].shape[1] - some, width)]
    more = () if into is None else (into,)
    return pl.pallas_call(
        functools.partial(stack_kernel, which),
        out_shape=[jax.ShapeDtypeStruct(shape, jnp.bfloat16) for shape in shapes],
        grid=(steps,),
        in_specs=specs + [pl.BlockSpec(memory_space=pl.ANY)] * len(more),
        out_specs=[pl.BlockSpec((UNROLL, rounds, 1, width, 2 * width), lambda n: (n, 0, which, 0, 0))] + [vmem] * (len(shapes) - 1),
        scratch_shapes=[] if which else [pltpu.SemaphoreType.DMA((2, 4))],
        input_output_aliases={len(specs): 0} if more else {},
        compiler_params=pltpu.CompilerParams(vmem_limit_bytes=24 << 20),
        cost_estimate=pl.CostEstimate(flops=20 * chosen * rounds * 2 * width * rows * width, bytes_accessed=8 << 20, transcendentals=0),
        name="stack" + str(which),
    )(side, first, mates, weight, norm, *parts, *more)


def per_device(spectra, counts, partner):
    bins, windows, parts, width = spectra.shape[1:]
    rounds, nblocks = partner.shape
    groups = lax.axis_size("yl") * lax.axis_size("core")
    chosen = nblocks // groups
    me = lax.axis_index(("yl", "core"))
    side = lax.axis_index("yh").reshape(1)
    first = me * chosen
    swap_pairs = [(0, 1), (1, 0)]
    after = lax.optimization_barrier

    def across(x):
        return lax.ppermute(x, "core", swap_pairs)

    def along(x):
        return lax.ppermute(x, "yl", swap_pairs)

    def hand_on(x):
        return lax.ppermute(x, ("yh", "yl"), [(0, 3), (3, 0), (1, 2), (2, 1)])

    shuffle = functools.partial(lax.all_to_all, axis_name=("x", "z"), split_axis=0, concat_axis=0, tiled=True)

    near, early, late = whiten(side, spectra.reshape(bins, windows * parts, width))
    beside = along(counts)
    tallies = (counts, across(counts), beside, across(beside))

    columns = jnp.concatenate(tallies, axis=0).astype(jnp.float32)
    mine = lax.dynamic_slice_in_dim(partner, first, chosen, 1)
    every = jnp.arange(nblocks, dtype=jnp.int32)[:, None]
    theirs_hot = (mine.T.reshape(1, chosen * rounds) == every).astype(jnp.float32)
    ours_hot = (first + jnp.arange(chosen * rounds, dtype=jnp.int32)[None] // rounds == every).astype(jnp.float32)
    pick = functools.partial(jnp.dot, precision=lax.Precision.HIGHEST)
    weight = jnp.minimum(pick(columns, ours_hot), pick(columns, theirs_hot)) / NSAMP
    norm = jnp.sqrt(jnp.sum(weight * weight, axis=0))
    steps = chosen // UNROLL
    wide = jnp.repeat(weight, parts, axis=0).reshape(-1, steps, UNROLL * rounds).transpose(1, 0, 2)

    near = shuffle(near)
    early, late = hand_on(early), hand_on(late)
    near, early, late, wide, norm = after((near, early, late, wide, norm))
    near_beside = along(near)
    near = (near, across(near), near_beside, across(near_beside))
    early = shuffle(early)
    late, near = after((late, near))
    early_beside = along(early)
    late = shuffle(late)
    late, early_beside = after((late, early_beside))
    late_beside = along(late)

    operands = (side, first.reshape(1), mine.reshape(-1), wide, norm)
    early = (early, across(early), early_beside, across(early_beside))
    result, near_kept, early_kept = stack(0, (*near, *early), *operands, None)
    late_beside, result = after((late_beside, result))
    late = (late, across(late), late_beside, across(late_beside))
    return stack(1, (near_kept, early_kept, *late), *operands, result)[0]


def solution(mesh):
    split = Mesh(mesh.devices.reshape(2, 4, 8, 2, 2), ("yh", "x", "z", "yl", "core"))
    chan, win = ("yh", "x", "z"), ("yl", "core")
    return jax.shard_map(
        per_device,
        mesh=split,
        in_specs=(P(chan, None, win, None, None), P(win, None), P()),
        out_specs=P(win, None, chan, None, None),
        check_vma=False,
    )
```

```python
import functools

import jax
import jax.numpy as jnp
from jax import lax
from jax.experimental import pallas as pl
from jax.experimental.pallas import tpu as pltpu
from jax.sharding import Mesh, PartitionSpec as P

NSAMP = 256
EPS = 1e-06
UNROLL = 8


def whiten_kernel(side_ref, x_ref, near_ref, early_ref, late_ref):
    bins, rows, width = x_ref.shape
    half = bins // 2
    more = early_ref.shape[1] - rows
    step = 4

    def add(i, total):
        for j in range(step):
            values = x_ref[i * step + j].astype(jnp.float32)
            total = total + values * values
        return total

    total = lax.fori_loop(0, bins // step, add, jnp.zeros((rows, width), jnp.float32))
    first = lax.broadcasted_iota(jnp.int32, (rows, width), 0) % 2 == 0
    other = jnp.where(first, pltpu.roll(total, rows - 1, 0), pltpu.roll(total, 1, 0))
    scale = lax.rsqrt((total + other) / bins + EPS)
    near = side_ref[0] * half
    far = half - near

    def put(i, carry):
        for j in range(step):
            at = i * step + j
            for which in range(2):
                near_ref[at, which] = (x_ref[near + 2 * at + which].astype(jnp.float32) * scale).astype(near_ref.dtype)
            early_ref[at, :rows] = (x_ref[far + 2 * at].astype(jnp.float32) * scale).astype(early_ref.dtype)
            odd = (x_ref[far + 2 * at + 1].astype(jnp.float32) * scale).astype(early_ref.dtype)
            early_ref[at, rows:] = odd[:more]
            late_ref[at] = odd[more:]
        return carry

    lax.fori_loop(0, half // 2 // step, put, 0)


def whiten(side, spectra):
    bins, rows, width = spectra.shape
    places = bins // 4
    vmem = pl.BlockSpec(memory_space=pltpu.VMEM)
    return pl.pallas_call(
        whiten_kernel,
        out_shape=[
            jax.ShapeDtypeStruct(shape, spectra.dtype)
            for shape in ((places, 2, rows, width), (places, rows + rows // 2, width), (places, rows // 2, width))
        ],
        in_specs=[pl.BlockSpec(memory_space=pltpu.SMEM), vmem],
        out_specs=[vmem] * 3,
        compiler_params=pltpu.CompilerParams(vmem_limit_bytes=16 << 20),
        name="whiten",
    )(side, spectra)


def turn_matrix(rows):
    i = lax.broadcasted_iota(jnp.int32, (rows, rows), 0)
    j = lax.broadcasted_iota(jnp.int32, (rows, rows), 1)
    plus = (i == j + 1) & (j % 2 == 0)
    minus = (i == j - 1) & (j % 2 == 1)
    return (plus.astype(jnp.float32) - minus.astype(jnp.float32)).astype(jnp.bfloat16)


def stack_kernel(which, side_ref, first_ref, mates_ref, weight_ref, norm_ref, *refs):
    rounds = weight_ref.shape[2] // UNROLL
    chosen = norm_ref.shape[0] // rounds
    side = side_ref[0]
    if which == 0:
        near, early, (out_ref, near_kept, early_kept, sems) = refs[:4], refs[4:8], refs[8:]
        half, _, rows, width = near[0].shape
        moves = [(near[t].at[:, 1], near_kept.at[t], sems.at[0, t]) for t in range(4)]
        moves += [(early[t].at[:, pl.ds(rows, early_kept.shape[2])], early_kept.at[t], sems.at[1, t]) for t in range(4)]

        @pl.when(pl.program_id(0) == 0)
        def keep():
            for move in moves:
                pltpu.make_async_copy(*move).start()
    else:
        near_kept, early_kept, late, out_ref = refs[0], refs[1], refs[2:6], refs[-1]
        half, rows, width = near_kept.shape[1:]

    def block(b):
        mine = b // half == side
        at = b % half
        parts = []
        for t in range(4):
            if which == 0:
                parts.append(jnp.where(mine, near[t][at, 0], early[t ^ 2][at, :rows]))
            else:
                far = jnp.concatenate([early_kept[t ^ 2, at], late[t ^ 2][at]], axis=0)
                parts.append(jnp.where(mine, near_kept[t, at], far))
        return jnp.concatenate(parts, axis=0)

    def weighted(x, column):
        return (x.astype(jnp.float32) * weight_ref[0, :, column : column + 1]).astype(x.dtype)

    turn = turn_matrix(4 * rows)
    for u in range(UNROLL):
        n = pl.program_id(0) * UNROLL + u
        own = block(first_ref[0] + n).T
        turned = jnp.dot(own, turn, preferred_element_type=jnp.float32).astype(own.dtype)
        left = jnp.concatenate([own, turned], axis=0)
        right = jnp.concatenate([weighted(block(mates_ref[r * chosen + n]), u * rounds + r) for r in range(rounds)], axis=1)
        both = jnp.dot(left, right, preferred_element_type=jnp.float32)
        for r in range(rounds):
            total = (both[:, r * width : (r + 1) * width] * (1.0 / norm_ref[n * rounds + r])).astype(out_ref.dtype)
            out_ref[u, r, 0, :, :width] = total[:width]
            out_ref[u, r, 0, :, width:] = total[width:]


    if which == 0:

        @pl.when(pl.program_id(0) == pl.num_programs(0) - 1)
        def kept():
            for move in moves:
                pltpu.make_async_copy(*move).wait()


def stack(which, parts, side, first, mates, weight, norm, into):
    steps, rows, columns = weight.shape
    chosen, rounds, width = steps * UNROLL, columns // UNROLL, parts[0].shape[-1]
    shapes = [(chosen, rounds, 2, width, 2 * width)]
    smem = pl.BlockSpec(memory_space=pltpu.SMEM)
    vmem = pl.BlockSpec(memory_space=pltpu.VMEM)
    specs = [smem, smem, smem, pl.BlockSpec((1, rows, columns), lambda n: (n, 0, 0)), smem] + [vmem] * len(parts)
    if which == 0:
        places, _, some = parts[0].shape[:3]
        shapes += [(4, places, some, width), (4, places, parts[4].shape[1] - some, width)]
    more = () if into is None else (into,)
    return pl.pallas_call(
        functools.partial(stack_kernel, which),
        out_shape=[jax.ShapeDtypeStruct(shape, jnp.bfloat16) for shape in shapes],
        grid=(steps,),
        in_specs=specs + [pl.BlockSpec(memory_space=pl.ANY)] * len(more),
        out_specs=[pl.BlockSpec((UNROLL, rounds, 1, width, 2 * width), lambda n: (n, 0, which, 0, 0))] + [vmem] * (len(shapes) - 1),
        scratch_shapes=[] if which else [pltpu.SemaphoreType.DMA((2, 4))],
        input_output_aliases={len(specs): 0} if more else {},
        compiler_params=pltpu.CompilerParams(vmem_limit_bytes=24 << 20),
        cost_estimate=pl.CostEstimate(flops=20 * chosen * rounds * 2 * width * rows * width, bytes_accessed=8 << 20, transcendentals=0),
        name="stack" + str(which),
    )(side, first, mates, weight, norm, *parts, *more)


def per_device(spectra, counts, partner):
    bins, windows, parts, width = spectra.shape[1:]
    rounds, nblocks = partner.shape
    groups = lax.axis_size("yl") * lax.axis_size("core")
    chosen = nblocks // groups
    me = lax.axis_index(("yl", "core"))
    side = lax.axis_index("yh").reshape(1)
    first = me * chosen
    swap_pairs = [(0, 1), (1, 0)]
    after = lax.optimization_barrier

    def across(x):
        return lax.ppermute(x, "core", swap_pairs)

    def along(x):
        return lax.ppermute(x, "yl", swap_pairs)

    def hand_on(x):
        return lax.ppermute(x, ("yh", "yl"), [(0, 3), (3, 0), (1, 2), (2, 1)])

    shuffle = functools.partial(lax.all_to_all, axis_name=("x", "z"), split_axis=0, concat_axis=0, tiled=True)

    near, early, late = whiten(side, spectra.reshape(bins, windows * parts, width))
    beside = along(counts)
    tallies = (counts, across(counts), beside, across(beside))

    columns = jnp.concatenate(tallies, axis=0).astype(jnp.float32)
    mine = lax.dynamic_slice_in_dim(partner, first, chosen, 1)
    every = jnp.arange(nblocks, dtype=jnp.int32)[:, None]
    theirs_hot = (mine.T.reshape(1, chosen * rounds) == every).astype(jnp.float32)
    ours_hot = (first + jnp.arange(chosen * rounds, dtype=jnp.int32)[None] // rounds == every).astype(jnp.float32)
    pick = functools.partial(jnp.dot, precision=lax.Precision.HIGHEST)
    weight = jnp.minimum(pick(columns, ours_hot), pick(columns, theirs_hot)) / NSAMP
    norm = jnp.sqrt(jnp.sum(weight * weight, axis=0))
    steps = chosen // UNROLL
    wide = jnp.repeat(weight, parts, axis=0).reshape(-1, steps, UNROLL * rounds).transpose(1, 0, 2)

    near = shuffle(near)
    early, late = hand_on(early), hand_on(late)
    near, early, wide, norm = after((near, early, wide, norm))
    near_beside, late = after((along(near), late))
    near = (near, across(near), near_beside, across(near_beside))
    early = shuffle(early)
    late, near = after((late, near))
    early_beside = along(early)
    late = shuffle(late)
    late, early_beside = after((late, early_beside))
    late_beside = along(late)

    operands = (side, first.reshape(1), mine.reshape(-1), wide, norm)
    early = (early, across(early), early_beside, across(early_beside))
    result, near_kept, early_kept = stack(0, (*near, *early), *operands, None)
    late_beside, result = after((late_beside, result))
    late = (late, across(late), late_beside, across(late_beside))
    return stack(1, (near_kept, early_kept, *late), *operands, result)[0]


def solution(mesh):
    split = Mesh(mesh.devices.reshape(2, 4, 8, 2, 2), ("yh", "x", "z", "yl", "core"))
    chan, win = ("yh", "x", "z"), ("yl", "core")
    return jax.shard_map(
        per_device,
        mesh=split,
        in_specs=(P(chan, None, win, None, None), P(win, None), P()),
        out_specs=P(win, None, chan, None, None),
        check_vma=False,
    )
```

```python
import functools

import jax
import jax.numpy as jnp
from jax import lax
from jax.experimental import pallas as pl
from jax.experimental.pallas import tpu as pltpu
from jax.sharding import Mesh, PartitionSpec as P

NSAMP = 256
EPS = 1e-06
UNROLL = 8


def whiten_kernel(side_ref, x_ref, near_ref, early_ref, late_ref):
    bins, rows, width = x_ref.shape
    half = bins // 2
    more = early_ref.shape[1] - rows
    step = 4

    def add(i, total):
        for j in range(step):
            values = x_ref[i * step + j].astype(jnp.float32)
            total = total + values * values
        return total

    total = lax.fori_loop(0, bins // step, add, jnp.zeros((rows, width), jnp.float32))
    first = lax.broadcasted_iota(jnp.int32, (rows, width), 0) % 2 == 0
    other = jnp.where(first, pltpu.roll(total, rows - 1, 0), pltpu.roll(total, 1, 0))
    scale = lax.rsqrt((total + other) / bins + EPS)
    near = side_ref[0] * half
    far = half - near

    def put(i, carry):
        for j in range(step):
            at = i * step + j
            for which in range(2):
                near_ref[at, which] = (x_ref[near + 2 * at + which].astype(jnp.float32) * scale).astype(near_ref.dtype)
            early_ref[at, :rows] = (x_ref[far + 2 * at].astype(jnp.float32) * scale).astype(early_ref.dtype)
            odd = (x_ref[far + 2 * at + 1].astype(jnp.float32) * scale).astype(early_ref.dtype)
            early_ref[at, rows:] = odd[:more]
            late_ref[at] = odd[more:]
        return carry

    lax.fori_loop(0, half // 2 // step, put, 0)


def whiten(side, spectra):
    bins, rows, width = spectra.shape
    places = bins // 4
    vmem = pl.BlockSpec(memory_space=pltpu.VMEM)
    return pl.pallas_call(
        whiten_kernel,
        out_shape=[
            jax.ShapeDtypeStruct(shape, spectra.dtype)
            for shape in ((places, 2, rows, width), (places, rows + rows // 2, width), (places, rows // 2, width))
        ],
        in_specs=[pl.BlockSpec(memory_space=pltpu.SMEM), vmem],
        out_specs=[vmem] * 3,
        compiler_params=pltpu.CompilerParams(vmem_limit_bytes=16 << 20),
        name="whiten",
    )(side, spectra)


def turn_matrix(rows):
    i = lax.broadcasted_iota(jnp.int32, (rows, rows), 0)
    j = lax.broadcasted_iota(jnp.int32, (rows, rows), 1)
    plus = (i == j + 1) & (j % 2 == 0)
    minus = (i == j - 1) & (j % 2 == 1)
    return (plus.astype(jnp.float32) - minus.astype(jnp.float32)).astype(jnp.bfloat16)


def stack_kernel(which, side_ref, first_ref, mates_ref, weight_ref, norm_ref, *refs):
    rounds = weight_ref.shape[2] // UNROLL
    chosen = norm_ref.shape[0] // rounds
    side = side_ref[0]
    if which == 0:
        near, early, (out_ref, near_kept, early_kept, held, sems) = refs[:4], refs[4:8], refs[8:]
        half, some = early_kept.shape[1:3]
        rows, width = held.shape[2:]
        here, there = pl.ds(side * half, half), pl.ds((1 - side) * half, half)
        now = [(near[t].at[:, 0], held.at[t, here], sems.at[0, t]) for t in range(4)]
        now += [(early[t ^ 2].at[:, pl.ds(0, rows)], held.at[t, there], sems.at[1, t]) for t in range(4)]
        later = [(near[t].at[:, 1], near_kept.at[t], sems.at[2, t]) for t in range(4)]
        later += [(early[t].at[:, pl.ds(rows, some)], early_kept.at[t], sems.at[3, t]) for t in range(4)]

        @pl.when(pl.program_id(0) == 0)
        def begin():
            for move in now:
                pltpu.make_async_copy(*move).start()
            for move in now:
                pltpu.make_async_copy(*move).wait()
            for move in later:
                pltpu.make_async_copy(*move).start()

    else:
        near_kept, early_kept, late, out_ref = refs[0], refs[1], refs[2:6], refs[-1]
        half, rows, width = near_kept.shape[1:]

    def block(b):
        mine = b // half == side
        at = b % half
        parts = []
        for t in range(4):
            if which == 0:
                parts.append(held[t, b])
            else:
                far = jnp.concatenate([early_kept[t ^ 2, at], late[t ^ 2][at]], axis=0)
                parts.append(jnp.where(mine, near_kept[t, at], far))
        return jnp.concatenate(parts, axis=0)

    def weighted(x, column):
        return (x.astype(jnp.float32) * weight_ref[0, :, column : column + 1]).astype(x.dtype)

    turn = turn_matrix(4 * rows)
    for u in range(UNROLL):
        n = pl.program_id(0) * UNROLL + u
        own = block(first_ref[0] + n).T
        turned = jnp.dot(own, turn, preferred_element_type=jnp.float32).astype(own.dtype)
        left = jnp.concatenate([own, turned], axis=0)
        right = jnp.concatenate([weighted(block(mates_ref[r * chosen + n]), u * rounds + r) for r in range(rounds)], axis=1)
        both = jnp.dot(left, right, preferred_element_type=jnp.float32)
        for r in range(rounds):
            total = (both[:, r * width : (r + 1) * width] * (1.0 / norm_ref[n * rounds + r])).astype(out_ref.dtype)
            out_ref[u, r, 0, :, :width] = total[:width]
            out_ref[u, r, 0, :, width:] = total[width:]


    if which == 0:

        @pl.when(pl.program_id(0) == pl.num_programs(0) - 1)
        def kept():
            for move in later:
                pltpu.make_async_copy(*move).wait()


def stack(which, parts, side, first, mates, weight, norm, into):
    steps, rows, columns = weight.shape
    chosen, rounds, width = steps * UNROLL, columns // UNROLL, parts[0].shape[-1]
    shapes = [(chosen, rounds, 2, width, 2 * width)]
    smem = pl.BlockSpec(memory_space=pltpu.SMEM)
    vmem = pl.BlockSpec(memory_space=pltpu.VMEM)
    anywhere = pl.BlockSpec(memory_space=pl.ANY)
    specs = [smem, smem, smem, pl.BlockSpec((1, rows, columns), lambda n: (n, 0, 0)), smem] + [vmem if which else anywhere] * len(parts)
    scratch = []
    if which == 0:
        places, _, some = parts[0].shape[:3]
        shapes += [(4, places, some, width), (4, places, parts[4].shape[1] - some, width)]
        scratch = [pltpu.VMEM((4, 2 * places, some, width), jnp.bfloat16), pltpu.SemaphoreType.DMA((4, 4))]
    more = () if into is None else (into,)
    return pl.pallas_call(
        functools.partial(stack_kernel, which),
        out_shape=[jax.ShapeDtypeStruct(shape, jnp.bfloat16) for shape in shapes],
        grid=(steps,),
        in_specs=specs + [anywhere] * len(more),
        out_specs=[pl.BlockSpec((UNROLL, rounds, 1, width, 2 * width), lambda n: (n, 0, which, 0, 0))] + [vmem] * (len(shapes) - 1),
        scratch_shapes=scratch,
        input_output_aliases={len(specs): 0} if more else {},
        compiler_params=pltpu.CompilerParams(vmem_limit_bytes=24 << 20),
        cost_estimate=pl.CostEstimate(flops=20 * chosen * rounds * 2 * width * rows * width, bytes_accessed=8 << 20, transcendentals=0),
        name="stack" + str(which),
    )(side, first, mates, weight, norm, *parts, *more)


def per_device(spectra, counts, partner):
    bins, windows, parts, width = spectra.shape[1:]
    rounds, nblocks = partner.shape
    groups = lax.axis_size("yl") * lax.axis_size("core")
    chosen = nblocks // groups
    me = lax.axis_index(("yl", "core"))
    side = lax.axis_index("yh").reshape(1)
    first = me * chosen
    swap_pairs = [(0, 1), (1, 0)]
    after = lax.optimization_barrier

    def across(x):
        return lax.ppermute(x, "core", swap_pairs)

    def along(x):
        return lax.ppermute(x, "yl", swap_pairs)

    def hand_on(x):
        return lax.ppermute(x, ("yh", "yl"), [(0, 3), (3, 0), (1, 2), (2, 1)])

    shuffle = functools.partial(lax.all_to_all, axis_name=("x", "z"), split_axis=0, concat_axis=0, tiled=True)

    near, early, late = whiten(side, spectra.reshape(bins, windows * parts, width))
    beside = along(counts)
    tallies = (counts, across(counts), beside, across(beside))

    columns = jnp.concatenate(tallies, axis=0).astype(jnp.float32)
    mine = lax.dynamic_slice_in_dim(partner, first, chosen, 1)
    every = jnp.arange(nblocks, dtype=jnp.int32)[:, None]
    theirs_hot = (mine.T.reshape(1, chosen * rounds) == every).astype(jnp.float32)
    ours_hot = (first + jnp.arange(chosen * rounds, dtype=jnp.int32)[None] // rounds == every).astype(jnp.float32)
    pick = functools.partial(jnp.dot, precision=lax.Precision.HIGHEST)
    weight = jnp.minimum(pick(columns, ours_hot), pick(columns, theirs_hot)) / NSAMP
    norm = jnp.sqrt(jnp.sum(weight * weight, axis=0))
    steps = chosen // UNROLL
    wide = jnp.repeat(weight, parts, axis=0).reshape(-1, steps, UNROLL * rounds).transpose(1, 0, 2)

    near = shuffle(near)
    early, late = hand_on(early), hand_on(late)
    near, early, wide, norm = after((near, early, wide, norm))
    near_beside, late = after((along(near), late))
    near = (near, across(near), near_beside, across(near_beside))
    early = shuffle(early)
    late, near = after((late, near))
    early_beside = along(early)
    late = shuffle(late)
    late, early_beside = after((late, early_beside))
    late_beside = along(late)

    operands = (side, first.reshape(1), mine.reshape(-1), wide, norm)
    early = (early, across(early), early_beside, across(early_beside))
    result, near_kept, early_kept = stack(0, (*near, *early), *operands, None)
    late_beside, result = after((late_beside, result))
    late = (late, across(late), late_beside, across(late_beside))
    return stack(1, (near_kept, early_kept, *late), *operands, result)[0]


def solution(mesh):
    split = Mesh(mesh.devices.reshape(2, 4, 8, 2, 2), ("yh", "x", "z", "yl", "core"))
    chan, win = ("yh", "x", "z"), ("yl", "core")
    return jax.shard_map(
        per_device,
        mesh=split,
        in_specs=(P(chan, None, win, None, None), P(win, None), P()),
        out_specs=P(win, None, chan, None, None),
        check_vma=False,
    )
```

```python
import functools

import jax
import jax.numpy as jnp
from jax import lax
from jax.experimental import pallas as pl
from jax.experimental.pallas import tpu as pltpu
from jax.sharding import Mesh, PartitionSpec as P

NSAMP = 256
EPS = 1e-06
UNROLL = 8


def near_kernel(side_ref, x_ref, near_ref, scale_ref, held, near, in_sems, out_sems):
    bins, rows, width = held.shape
    half = bins // 2
    step = 4
    slabs, parts = in_sems.shape[0], out_sems.shape[0]
    slab, part = bins // slabs, half // 2 // parts
    loads = [pltpu.make_async_copy(x_ref.at[pl.ds(i * slab, slab)], held.at[pl.ds(i * slab, slab)], in_sems.at[i]) for i in range(slabs)]
    for load in loads:
        load.start()

    def add(i, total):
        for j in range(step):
            values = held[i * step + j].astype(jnp.float32)
            total = total + values * values
        return total

    total = jnp.zeros((rows, width), jnp.float32)
    for i, load in enumerate(loads):
        load.wait()
        total = lax.fori_loop(i * slab // step, (i + 1) * slab // step, add, total)
    first = lax.broadcasted_iota(jnp.int32, (rows, width), 0) % 2 == 0
    other = jnp.where(first, pltpu.roll(total, rows - 1, 0), pltpu.roll(total, 1, 0))
    scale = lax.rsqrt((total + other) / bins + EPS)
    scale_ref[...] = scale
    here = side_ref[0] * half

    def put(i, carry):
        for j in range(step):
            for which in range(2):
                at = i * step + j
                near[at, which] = (held[here + 2 * at + which].astype(jnp.float32) * scale).astype(near.dtype)
        return carry

    stores = []
    for i in range(parts):
        lax.fori_loop(i * part // step, (i + 1) * part // step, put, 0)
        places = pl.ds(i * part, part)
        stores.append(pltpu.make_async_copy(near.at[places], near_ref.at[places], out_sems.at[i]))
        stores[-1].start()
    for store in stores:
        store.wait()


def far_kernel(side_ref, x_ref, scale_ref, early_ref, late_ref, held, sem):
    half, rows, width = held.shape
    more = early_ref.shape[1] - rows
    step = 4
    load = pltpu.make_async_copy(x_ref.at[pl.ds((1 - side_ref[0]) * half, half)], held, sem)
    load.start()
    load.wait()
    scale = scale_ref[...]

    def put(i, carry):
        for j in range(step):
            at = i * step + j
            early_ref[at, :rows] = (held[2 * at].astype(jnp.float32) * scale).astype(early_ref.dtype)
            odd = (held[2 * at + 1].astype(jnp.float32) * scale).astype(early_ref.dtype)
            early_ref[at, rows:] = odd[:more]
            late_ref[at] = odd[more:]
        return carry

    lax.fori_loop(0, half // 2 // step, put, 0)


def whiten(side, spectra):
    bins, rows, width = spectra.shape
    places = bins // 4
    smem = pl.BlockSpec(memory_space=pltpu.SMEM)
    vmem = pl.BlockSpec(memory_space=pltpu.VMEM)
    params = pltpu.CompilerParams(vmem_limit_bytes=16 << 20)
    near, scale = pl.pallas_call(
        near_kernel,
        out_shape=[jax.ShapeDtypeStruct((places, 2, rows, width), spectra.dtype), jax.ShapeDtypeStruct((rows, width), jnp.float32)],
        in_specs=[smem, pl.BlockSpec(memory_space=pl.ANY)],
        out_specs=[pl.BlockSpec(memory_space=pl.ANY), vmem],
        scratch_shapes=[
            pltpu.VMEM(spectra.shape, spectra.dtype),
            pltpu.VMEM((places, 2, rows, width), spectra.dtype),
            pltpu.SemaphoreType.DMA((8,)),
            pltpu.SemaphoreType.DMA((4,)),
        ],
        compiler_params=pltpu.CompilerParams(vmem_limit_bytes=61 << 20),
        name="whiten_near",
    )(side, spectra)
    shapes = ((places, rows + rows // 2, width), (places, rows // 2, width))
    early, late = pl.pallas_call(
        far_kernel,
        out_shape=[jax.ShapeDtypeStruct(shape, spectra.dtype) for shape in shapes],
        in_specs=[smem, pl.BlockSpec(memory_space=pl.ANY), vmem],
        out_specs=[vmem] * 2,
        scratch_shapes=[pltpu.VMEM((bins // 2, rows, width), spectra.dtype), pltpu.SemaphoreType.DMA],
        compiler_params=params,
        cost_estimate=pl.CostEstimate(flops=0, bytes_accessed=4 << 20, transcendentals=0),
        name="whiten_far",
    )(side, spectra, scale)
    return near, early, late


def turn_matrix(rows):
    i = lax.broadcasted_iota(jnp.int32, (rows, rows), 0)
    j = lax.broadcasted_iota(jnp.int32, (rows, rows), 1)
    plus = (i == j + 1) & (j % 2 == 0)
    minus = (i == j - 1) & (j % 2 == 1)
    return (plus.astype(jnp.float32) - minus.astype(jnp.float32)).astype(jnp.bfloat16)


def stack_kernel(which, side_ref, first_ref, mates_ref, weight_ref, norm_ref, *refs):
    rounds = weight_ref.shape[2] // UNROLL
    chosen = norm_ref.shape[0] // rounds
    side = side_ref[0]
    if which == 0:
        near, early, (out_ref, near_kept, early_kept, held, sems) = refs[:4], refs[4:8], refs[8:]
        half, some = early_kept.shape[1:3]
        rows, width = held.shape[2:]
        here, there = pl.ds(side * half, half), pl.ds((1 - side) * half, half)
        now = [(near[t].at[:, 0], held.at[t, here], sems.at[0, t]) for t in range(4)]
        now += [(early[t ^ 2].at[:, pl.ds(0, rows)], held.at[t, there], sems.at[1, t]) for t in range(4)]
        later = [(near[t].at[:, 1], near_kept.at[t], sems.at[2, t]) for t in range(4)]
        later += [(early[t].at[:, pl.ds(rows, some)], early_kept.at[t], sems.at[3, t]) for t in range(4)]

        @pl.when(pl.program_id(0) == 0)
        def begin():
            for move in now:
                pltpu.make_async_copy(*move).start()
            for move in now:
                pltpu.make_async_copy(*move).wait()
            for move in later:
                pltpu.make_async_copy(*move).start()

    else:
        near_kept, early_kept, late, out_ref = refs[0], refs[1], refs[2:6], refs[-1]
        half, rows, width = near_kept.shape[1:]

    def block(b):
        mine = b // half == side
        at = b % half
        parts = []
        for t in range(4):
            if which == 0:
                parts.append(held[t, b])
            else:
                far = jnp.concatenate([early_kept[t ^ 2, at], late[t ^ 2][at]], axis=0)
                parts.append(jnp.where(mine, near_kept[t, at], far))
        return jnp.concatenate(parts, axis=0)

    def weighted(x, column):
        return (x.astype(jnp.float32) * weight_ref[0, :, column : column + 1]).astype(x.dtype)

    turn = turn_matrix(4 * rows)
    for u in range(UNROLL):
        n = pl.program_id(0) * UNROLL + u
        own = block(first_ref[0] + n).T
        turned = jnp.dot(own, turn, preferred_element_type=jnp.float32).astype(own.dtype)
        left = jnp.concatenate([own, turned], axis=0)
        right = jnp.concatenate([weighted(block(mates_ref[r * chosen + n]), u * rounds + r) for r in range(rounds)], axis=1)
        both = jnp.dot(left, right, preferred_element_type=jnp.float32)
        for r in range(rounds):
            total = (both[:, r * width : (r + 1) * width] * (1.0 / norm_ref[n * rounds + r])).astype(out_ref.dtype)
            out_ref[u, r, 0, :, :width] = total[:width]
            out_ref[u, r, 0, :, width:] = total[width:]


    if which == 0:

        @pl.when(pl.program_id(0) == pl.num_programs(0) - 1)
        def kept():
            for move in later:
                pltpu.make_async_copy(*move).wait()


def stack(which, parts, side, first, mates, weight, norm, into):
    steps, rows, columns = weight.shape
    chosen, rounds, width = steps * UNROLL, columns // UNROLL, parts[0].shape[-1]
    shapes = [(chosen, rounds, 2, width, 2 * width)]
    smem = pl.BlockSpec(memory_space=pltpu.SMEM)
    vmem = pl.BlockSpec(memory_space=pltpu.VMEM)
    anywhere = pl.BlockSpec(memory_space=pl.ANY)
    specs = [smem, smem, smem, pl.BlockSpec((1, rows, columns), lambda n: (n, 0, 0)), smem] + [vmem if which else anywhere] * len(parts)
    scratch = []
    if which == 0:
        places, _, some = parts[0].shape[:3]
        shapes += [(4, places, some, width), (4, places, parts[4].shape[1] - some, width)]
        scratch = [pltpu.VMEM((4, 2 * places, some, width), jnp.bfloat16), pltpu.SemaphoreType.DMA((4, 4))]
    more = () if into is None else (into,)
    return pl.pallas_call(
        functools.partial(stack_kernel, which),
        out_shape=[jax.ShapeDtypeStruct(shape, jnp.bfloat16) for shape in shapes],
        grid=(steps,),
        in_specs=specs + [anywhere] * len(more),
        out_specs=[pl.BlockSpec((UNROLL, rounds, 1, width, 2 * width), lambda n: (n, 0, which, 0, 0))] + [vmem] * (len(shapes) - 1),
        scratch_shapes=scratch,
        input_output_aliases={len(specs): 0} if more else {},
        compiler_params=pltpu.CompilerParams(vmem_limit_bytes=24 << 20),
        cost_estimate=pl.CostEstimate(flops=20 * chosen * rounds * 2 * width * rows * width, bytes_accessed=8 << 20, transcendentals=0),
        name="stack" + str(which),
    )(side, first, mates, weight, norm, *parts, *more)


def per_device(spectra, counts, partner):
    bins, windows, parts, width = spectra.shape[1:]
    rounds, nblocks = partner.shape
    groups = lax.axis_size("yl") * lax.axis_size("core")
    chosen = nblocks // groups
    me = lax.axis_index(("yl", "core"))
    side = lax.axis_index("yh").reshape(1)
    first = me * chosen
    swap_pairs = [(0, 1), (1, 0)]
    after = lax.optimization_barrier

    def across(x):
        return lax.ppermute(x, "core", swap_pairs)

    def along(x):
        return lax.ppermute(x, "yl", swap_pairs)

    def hand_on(x):
        return lax.ppermute(x, ("yh", "yl"), [(0, 3), (3, 0), (1, 2), (2, 1)])

    shuffle = functools.partial(lax.all_to_all, axis_name=("x", "z"), split_axis=0, concat_axis=0, tiled=True)

    near, early, late = whiten(side, spectra.reshape(bins, windows * parts, width))
    beside = along(counts)
    tallies = (counts, across(counts), beside, across(beside))

    columns = jnp.concatenate(tallies, axis=0).astype(jnp.float32)
    mine = lax.dynamic_slice_in_dim(partner, first, chosen, 1)
    every = jnp.arange(nblocks, dtype=jnp.int32)[:, None]
    theirs_hot = (mine.T.reshape(1, chosen * rounds) == every).astype(jnp.float32)
    ours_hot = (first + jnp.arange(chosen * rounds, dtype=jnp.int32)[None] // rounds == every).astype(jnp.float32)
    pick = functools.partial(jnp.dot, precision=lax.Precision.HIGHEST)
    weight = jnp.minimum(pick(columns, ours_hot), pick(columns, theirs_hot)) / NSAMP
    norm = jnp.sqrt(jnp.sum(weight * weight, axis=0))
    steps = chosen // UNROLL
    wide = jnp.repeat(weight, parts, axis=0).reshape(-1, steps, UNROLL * rounds).transpose(1, 0, 2)

    near = shuffle(near)
    early, late = hand_on(early), hand_on(late)
    near, early, wide, norm = after((near, early, wide, norm))
    near_beside, late = after((along(near), late))
    near = (near, across(near), near_beside, across(near_beside))
    early = shuffle(early)
    late, near = after((late, near))
    early_beside = along(early)
    late = shuffle(late)
    late, early_beside = after((late, early_beside))
    late_beside = along(late)

    operands = (side, first.reshape(1), mine.reshape(-1), wide, norm)
    early = (early, across(early), early_beside, across(early_beside))
    result, near_kept, early_kept = stack(0, (*near, *early), *operands, None)
    late_beside, result = after((late_beside, result))
    late = (late, across(late), late_beside, across(late_beside))
    return stack(1, (near_kept, early_kept, *late), *operands, result)[0]


def solution(mesh):
    split = Mesh(mesh.devices.reshape(2, 4, 8, 2, 2), ("yh", "x", "z", "yl", "core"))
    chan, win = ("yh", "x", "z"), ("yl", "core")
    return jax.shard_map(
        per_device,
        mesh=split,
        in_specs=(P(chan, None, win, None, None), P(win, None), P()),
        out_specs=P(win, None, chan, None, None),
        check_vma=False,
    )
```
